32 devices in a mesh: blk: 8 (over z, y), gy: 4 (over x, core).
Axes of the slice: x: 2, y: 2, z: 4, core: 2. Of those that a mesh axis runs over, the one named last changes fastest.
Arguments:
- image: float32 [1, 2048, 2048], P(None, 'blk', 'gy'), may hold values from -6 to 6
- measured: float32 [1, 16, 2816], P(None, 'blk'), may hold values from -6 to 6
- row_weight: float32 [16, 2816], P('blk'), may hold values from 0.25 to 2
- col_weight: float32 [2048, 2048], P('blk', 'gy'), may hold values from 1 to 8
- band_weight: bfloat16 [16, 2048, 128], P('blk', 'gy'), may hold values from -0.01171875 to 0.01171875
- band_shift: int32 [16, 8], replicated, may hold values from 0 to 3
Outputs:
- updated: float32 [1, 2048, 2048], P(None, 'blk', 'gy')
The draws below stay inside these ranges and needn't reach their ends.
Inputs may be any that keep to these rules, and one draw needn't show every extreme that they name: band_shift[t, s] is the number of panels by which slab s's footprint under tilt t starts beyond panel s * 2.
All inputs are finite; a program needn't handle non-finite values.
Results may differ from the reference program's by a relative error of at most 0.0025.
Values may be sent and summed in bfloat16 or wider, within the bound.
A program may use at most 64 MiB of HBM per device.

```python
import math
import jax
import jax.numpy as jnp
from jax import lax

XS = 256
NY = 1
BW = 128
PW = 128
Z = 2048
NT = 16
NX = 2048
FP = 3
NU = 2816
N_BLK = 8


def plant(drawn, own_key, smallest, top_value):
    spot = [jax.random.randint(jax.random.fold_in(own_key, axis), (), 0, length) for axis, length in enumerate(drawn.shape)]
    longest = drawn.shape.index(max(drawn.shape))
    next_to = spot[:longest] + [(spot[longest] + 1) % drawn.shape[longest]] + spot[longest + 1:]
    return drawn.at[tuple(spot)].set(smallest).at[tuple(next_to)].set(top_value)


def level_of(stream_key, shape, shards, smallest, high):
    loudness, own = 1.0, jax.random.fold_in(stream_key, 6)
    for position, blocks in shards:
        steps = jnp.exp(jax.random.uniform(jax.random.fold_in(own, position), (blocks,), jnp.float32, smallest / len(shards), high / len(shards)))
        loudness = loudness * jnp.repeat(steps, shape[position] // blocks).reshape([-1 if axis == position else 1 for axis in range(len(shape))])
    return loudness


def bell_draw(own_key, dims, deviation, limit, shards=(), held_as=jnp.bfloat16):
    array = jax.random.normal(own_key, dims, jnp.float32) * deviation
    if len(shards) > 0:
        array = level_of(own_key, dims, shards, -0.22, 0.18) * array
    return jnp.clip(array, min=-limit, max=limit).astype(held_as)


def setup_inputs(seed: int = 0) -> dict:
    splits = jax.random.split(jax.random.key(seed), 7)
    image = bell_draw(splits[0], (NY, NX, Z), 1.0, 6.0, ((1, 8), (2, 4)), jnp.float32)
    measured = bell_draw(splits[1], (NY, NT, NU), 1.0, 6.0, ((1, 8),), jnp.float32)
    row_weight = jnp.clip(jnp.exp(math.log(2.0) - 2.0794415 * jax.random.uniform(splits[2], (NT, NU), jnp.float32) ** level_of(splits[2], (NT, NU), ((0, 8),), -0.2, 0.2)), 0.25, 2.0)
    col_weight = jnp.clip(jnp.exp(math.log(8.0) - 2.0794415 * jax.random.uniform(splits[3], (NX, Z), jnp.float32) ** level_of(splits[3], (NX, Z), ((0, 8), (1, 4)), -0.2, 0.2)), 1.0, 8.0)
    band_weight = bell_draw(splits[4], (NT, Z, BW), (Z * BW) ** -0.5, 0.01171875, ((0, 8), (1, 4)))
    band_shift = plant(jax.random.randint(splits[5], (NT, N_BLK), 0, FP + 1), jax.random.fold_in(splits[5], 1), 0, FP).astype(jnp.int32)
    return dict(image=image, measured=measured, row_weight=row_weight, col_weight=col_weight, band_weight=band_weight, band_shift=band_shift)


SMOOTH = 0.25


def reference(image, measured, row_weight, col_weight, band_weight, band_shift):
    row_count = image.shape[0]
    depth = image.shape[2]
    window_len = XS + BW
    rounded = lax.optimization_barrier(image.astype(jnp.bfloat16))
    copies = rounded.astype(jnp.float32).reshape(row_count, N_BLK, XS, depth)
    slab_bins = ((jnp.arange(N_BLK, dtype=jnp.int32) * (XS // PW))[None, :] + band_shift) * PW
    offsets = jnp.arange(window_len, dtype=jnp.int32)
    diag_index = (jnp.arange(XS)[:, None] + jnp.arange(BW)[None, :]).astype(jnp.int32)

    def forward_tilt(operands):
        weights, bins = operands
        product = jnp.einsum("ysiz,zd->ysid", copies, weights.astype(jnp.float32))
        windows = jnp.zeros((row_count, N_BLK, window_len), jnp.float32).at[:, :, diag_index].add(product)
        target = bins[:, None] + offsets[None, :]
        return jnp.zeros((row_count, NU), jnp.float32).at[:, target].add(windows)

    projection = lax.map(forward_tilt, (band_weight, slab_bins))
    projection = jnp.transpose(projection, (1, 0, 2))
    weighted = (row_weight[None] * (measured - projection)).astype(jnp.bfloat16)

    def back_tilt(running, operands):
        detector_line, weights, bins = operands
        target = bins[:, None] + offsets[None, :]
        panels = detector_line[:, target]
        sheared = panels[:, :, diag_index]
        added = jnp.einsum("ysid,zd->ysiz", sheared.astype(jnp.float32), weights.astype(jnp.float32))
        return running + added, None

    initial = jnp.zeros((row_count, N_BLK, XS, depth), jnp.float32)
    backed, leftover = lax.scan(back_tilt, initial, (jnp.transpose(weighted, (1, 0, 2)), band_weight, slab_bins))
    backed = backed.reshape(row_count, N_BLK * XS, depth)
    padded = jnp.pad(image, ((0, 0), (0, 0), (1, 1)))
    return image + col_weight[None] * backed + SMOOTH * (padded[:, :, :-2] + padded[:, :, 2:] - 2.0 * image)
```

```python
import functools

import jax
import jax.numpy as jnp
from jax import lax
from jax.experimental import pallas as pl
from jax.experimental.pallas import tpu as pltpu
from jax.sharding import PartitionSpec as P

PW = 128
SMOOTH = 0.25
SHIFTS = 4
MESH = pl.DeviceIdType.MESH


def roll_lanes(rows, amount):
    return pltpu.roll(rows, amount % rows.shape[1], 1)


def diagonal_sum(product):
    parts = [product[c : c + PW] for c in range(0, product.shape[0], PW)]
    rows = jnp.concatenate(parts + [jnp.zeros((PW, PW), jnp.float32)], axis=1)
    half = PW // 2
    while half >= 8:
        rows = rows[:half] + roll_lanes(rows[half:], half)
        half //= 2
    sub = lax.broadcasted_iota(jnp.int32, rows.shape, 0)
    for level in (4, 2, 1):
        rows = jnp.where(sub & level != 0, roll_lanes(rows, level), rows)
    return jnp.sum(rows, axis=0, keepdims=True)


def band_rows(line, col_count):
    rows = jnp.broadcast_to(line, (8, line.shape[1]))
    sub = lax.broadcasted_iota(jnp.int32, rows.shape, 0)
    for level in (4, 2, 1):
        rows = jnp.where(sub & level != 0, roll_lanes(rows, -level), rows)
    while rows.shape[0] < PW:
        rows = jnp.concatenate([rows, roll_lanes(rows, -rows.shape[0])], axis=0)
    return jnp.concatenate([rows[:, c : c + PW] for c in range(0, col_count, PW)], axis=0)


def kernel(
    blocks, groups,
    image_ref, measured_ref, row_ref, col_ref, band_ref, shift_ref, out_ref,
    weights, copies, shift_rows, placed, footprints, partial, cut, panels, edge_out, edge_in,
    up_sem, down_sem, side_sem, weight_sem,
    foot_send, foot_recv, part_send, part_recv, cut_send, cut_recv, edge_send, edge_recv,
):
    blk, gy = lax.axis_index("blk"), lax.axis_index("gy")
    line = blocks // 2
    spot, side = blk // 2, blk % 2
    local_tilts, depth, band_width = band_ref.shape
    col_count = image_ref.shape[0]
    detector_len = measured_ref.shape[1]
    per_slab = col_count // PW
    window_panels = per_slab + 1
    reach = window_panels + SHIFTS - 1

    edge_in[...] = jnp.zeros_like(edge_in)
    barrier = pltpu.get_barrier_semaphore()

    def greet_blk(step, carry):
        peer = lax.rem(blk + step, blocks)
        pl.semaphore_signal(barrier, inc=1, device_id=(peer, gy), device_id_type=MESH)
        return carry

    def greet_gy(step, carry):
        peer = lax.rem(gy + step, groups)
        pl.semaphore_signal(barrier, inc=1, device_id=(blk, peer), device_id_type=MESH)
        return carry

    lax.fori_loop(1, blocks, greet_blk, 0)
    lax.fori_loop(1, groups, greet_gy, 0)
    pl.semaphore_wait(barrier, blocks + groups - 2)

    def send_weights(block, sems, to):
        return pltpu.make_async_remote_copy(
            src_ref=weights.at[block], dst_ref=weights.at[block],
            send_sem=sems.at[block], recv_sem=weight_sem.at[block],
            device_id=(to, gy), device_id_type=MESH,
        )

    def send_up(block):
        return send_weights(block, up_sem, lax.rem(blk + 2, blocks))

    def send_down(block):
        return send_weights(block, down_sem, lax.rem(blk + blocks - 2, blocks))

    def send_side(block):
        return send_weights(block, side_sem, blk + 1 - 2 * side)

    def send_foot(block):
        return pltpu.make_async_remote_copy(
            src_ref=placed.at[block], dst_ref=footprints.at[blk],
            send_sem=foot_send.at[block], recv_sem=foot_recv.at[blk],
            device_id=(block, gy), device_id_type=MESH,
        )

    def foot_from(block):
        return pltpu.make_async_remote_copy(
            src_ref=placed.at[block], dst_ref=footprints.at[block],
            send_sem=foot_send.at[block], recv_sem=foot_recv.at[block],
            device_id=(block, gy), device_id_type=MESH,
        )

    def edge_copy(which, to):
        return pltpu.make_async_remote_copy(
            src_ref=edge_out.at[which], dst_ref=edge_in.at[which, pl.ds(0, 8)],
            send_sem=edge_send.at[which], recv_sem=edge_recv.at[which],
            device_id=(blk, to), device_id_type=MESH,
        )

    def tail_copy():
        return edge_copy(0, lax.rem(gy + 1, groups))

    def head_copy():
        return edge_copy(1, lax.rem(gy + groups - 1, groups))

    weights[blk] = band_ref[...]

    @pl.when(spot < line - 1)
    def _():
        send_up(blk).start()

    @pl.when(spot > 0)
    def _():
        send_down(blk).start()

    send_side(blk).start()

    copies[...] = image_ref[...].astype(jnp.bfloat16)
    slab = lax.broadcasted_iota(jnp.int32, shift_ref.shape, 1)
    own_shift = jnp.sum(jnp.where(slab == blk, shift_ref[...], 0), axis=1, keepdims=True)
    shift_rows[...] = jnp.broadcast_to(own_shift, shift_rows.shape)

    edge_out[0] = image_ref[:, depth - PW :].T[PW - 8 :]
    edge_out[1] = image_ref[:, :PW].T[:8]

    @pl.when(gy < groups - 1)
    def _():
        tail_copy().start()

    @pl.when(gy > 0)
    def _():
        head_copy().start()

    def wide(block):
        return jnp.concatenate([weights[block, t] for t in range(local_tilts)], axis=1)

    def project(block):
        product = jnp.dot(copies[...], wide(block), preferred_element_type=jnp.float32)
        for t in range(local_tilts):
            window = diagonal_sum(product[:, t * band_width : (t + 1) * band_width])
            shift = shift_rows[pl.ds(block * local_tilts + t, 1), :]
            for panel in range(reach):
                total = jnp.zeros((1, PW), jnp.float32)
                for k in range(SHIFTS):
                    if 0 <= panel - k < window_panels:
                        piece = window[:, (panel - k) * PW : (panel - k + 1) * PW]
                        total = jnp.where(shift == k, piece, total)
                placed[block, pl.ds(t, 1), pl.ds(panel * PW, PW)] = total

        @pl.when(block != blk)
        def _():
            send_foot(block).start()

        @pl.when(block == blk)
        def _():
            footprints[blk] = placed[blk]

    def gather_step(step, carry):
        below, above = spot - step, spot + step

        @pl.when((step > 0) & (below >= 0))
        def _():
            block = below * 2 + side
            send_up(block).wait_recv()

            @pl.when(spot < line - 1)
            def _():
                send_up(block).start()

            send_side(block).start()

        @pl.when((step > 0) & (above < line))
        def _():
            block = above * 2 + side
            send_down(block).wait_recv()

            @pl.when(spot > 0)
            def _():
                send_down(block).start()

            send_side(block).start()

        def visit(turn, carry):
            other = turn // 2
            far = step - other
            place = jnp.where(turn % 2 == 0, spot - far, spot + far)
            inside = (far >= 0) & (place >= 0) & (place < line) & ((far > 0) | (turn % 2 == 0))
            block = place * 2 + jnp.where(other == 0, side, 1 - side)

            @pl.when(inside)
            def _():
                @pl.when(other == 1)
                def _():
                    send_side(block).wait_recv()

                project(block)

            return carry

        return lax.fori_loop(0, 4, visit, carry)

    lax.fori_loop(0, line + 1, gather_step, 0)

    def take_foot(step, carry):
        foot_from(lax.rem(blk + step, blocks)).wait_recv()
        return carry

    lax.fori_loop(1, blocks, take_foot, 0)

    partial[gy] = jnp.zeros((local_tilts, detector_len), jnp.float32)
    for source in range(blocks):
        bins = pl.ds(source * per_slab * PW, reach * PW)
        partial[gy, :, bins] = partial[gy, :, bins] + footprints[source]

    def part_copy(to, slot):
        return pltpu.make_async_remote_copy(
            src_ref=partial.at[gy], dst_ref=partial.at[slot],
            send_sem=part_send.at[to], recv_sem=part_recv.at[slot],
            device_id=(blk, to), device_id_type=MESH,
        )

    def give_part(step, carry):
        part_copy(lax.rem(gy + step, groups), gy).start()
        return carry

    def take_part(step, carry):
        peer = lax.rem(gy + step, groups)
        part_copy(peer, peer).wait_recv()
        return carry

    lax.fori_loop(1, groups, give_part, 0)
    lax.fori_loop(1, groups, take_part, 0)

    projection = partial[0]
    for group in range(1, groups):
        projection = projection + partial[group]
    weighted = (row_ref[...] * (measured_ref[...] - projection)).astype(jnp.bfloat16)
    weighted = weighted.astype(jnp.float32)
    for block in range(blocks):
        start = block * per_slab * PW
        cut[block] = weighted[:, start : start + reach * PW]

    def cut_copy(to, slot):
        return pltpu.make_async_remote_copy(
            src_ref=cut.at[to], dst_ref=panels.at[slot],
            send_sem=cut_send.at[to], recv_sem=cut_recv.at[slot],
            device_id=(to, gy), device_id_type=MESH,
        )

    def give_cut(step, carry):
        cut_copy(lax.rem(blk + step, blocks), blk).start()
        return carry

    lax.fori_loop(1, blocks, give_cut, 0)
    panels[blk] = cut[blk]
    out_ref[...] = jnp.zeros_like(out_ref)

    def back_step(step, carry):
        source = lax.rem(blk + step, blocks)

        @pl.when(step > 0)
        def _():
            cut_copy(source, source).wait_recv()

        sheared = []
        for t in range(local_tilts):
            shift = shift_rows[pl.ds(source * local_tilts + t, 1), :]
            pieces = []
            for panel in range(window_panels):
                piece = panels[source, pl.ds(t, 1), pl.ds(panel * PW, PW)]
                for k in range(1, SHIFTS):
                    moved = panels[source, pl.ds(t, 1), pl.ds((panel + k) * PW, PW)]
                    piece = jnp.where(shift == k, moved, piece)
                pieces.append(piece)
            sheared.append(band_rows(jnp.concatenate(pieces, axis=1), col_count))
        rows = jnp.concatenate(sheared, axis=1).astype(jnp.bfloat16)
        out_ref[...] += lax.dot_general(
            rows, wide(source), (((1,), (1,)), ((), ())), preferred_element_type=jnp.float32
        )
        return carry

    lax.fori_loop(0, blocks, back_step, 0)

    @pl.when(gy > 0)
    def _():
        tail_copy().wait_recv()

    @pl.when(gy < groups - 1)
    def _():
        head_copy().wait_recv()

    before = edge_in[0].T[:, 7:8]
    after = edge_in[1].T[:, 0:1]
    chunk = 32
    lane = lax.broadcasted_iota(jnp.int32, (chunk, depth), 1)
    for top in range(0, col_count, chunk):
        rows = slice(top, top + chunk)
        here = image_ref[rows, :]
        left = jnp.where(lane == 0, before[rows], roll_lanes(here, 1))
        right = jnp.where(lane == depth - 1, after[rows], roll_lanes(here, -1))
        out_ref[rows, :] = (
            here + col_ref[rows, :] * out_ref[rows, :] + SMOOTH * (left + right - 2.0 * here)
        )

    @pl.when(gy < groups - 1)
    def _():
        tail_copy().wait_send()

    @pl.when(gy > 0)
    def _():
        head_copy().wait_send()

    def settle_line(place, carry):
        block = place * 2 + side

        @pl.when((place <= spot) & (spot < line - 1))
        def _():
            send_up(block).wait_send()

        @pl.when((place >= spot) & (spot > 0))
        def _():
            send_down(block).wait_send()

        send_side(block).wait_send()
        return carry

    def settle_blk(step, carry):
        peer = lax.rem(blk + step, blocks)
        send_foot(peer).wait_send()
        cut_copy(peer, blk).wait_send()
        return carry

    def settle_gy(step, carry):
        part_copy(lax.rem(gy + step, groups), gy).wait_send()
        return carry

    lax.fori_loop(0, line, settle_line, 0)
    lax.fori_loop(1, blocks, settle_blk, 0)
    lax.fori_loop(1, groups, settle_gy, 0)


def per_device(blocks, groups, image, measured, row_weight, col_weight, band_weight, band_shift):
    _, col_count, depth = image.shape
    local_tilts, _, band_width = band_weight.shape
    detector_len = measured.shape[2]
    reach = (col_count // PW + SHIFTS) * PW
    window = (blocks, local_tilts, reach)
    dma = pltpu.SemaphoreType.DMA
    updated = pl.pallas_call(
        functools.partial(kernel, blocks, groups),
        out_shape=jax.ShapeDtypeStruct((col_count, depth), jnp.float32),
        in_specs=[pl.BlockSpec(memory_space=pltpu.VMEM)] * 6,
        out_specs=pl.BlockSpec(memory_space=pltpu.VMEM),
        scratch_shapes=[
            pltpu.VMEM((blocks,) + band_weight.shape, jnp.bfloat16),
            pltpu.VMEM((col_count, depth), jnp.bfloat16),
            pltpu.VMEM((blocks * local_tilts, PW), jnp.int32),
            pltpu.VMEM(window, jnp.float32),
            pltpu.VMEM(window, jnp.float32),
            pltpu.VMEM((groups, local_tilts, detector_len), jnp.float32),
            pltpu.VMEM(window, jnp.float32),
            pltpu.VMEM(window, jnp.float32),
            pltpu.VMEM((2, 8, col_count), jnp.float32),
            pltpu.VMEM((2, PW, col_count), jnp.float32),
            dma((blocks,)), dma((blocks,)), dma((blocks,)), dma((blocks,)),
            dma((blocks,)), dma((blocks,)), dma((groups,)), dma((groups,)),
            dma((blocks,)), dma((blocks,)), dma((2,)), dma((2,)),
        ],
        compiler_params=pltpu.CompilerParams(
            collective_id=0, has_side_effects=True, vmem_limit_bytes=40 * 1024 * 1024
        ),
        cost_estimate=pl.CostEstimate(
            flops=4 * blocks * local_tilts * band_width * col_count * depth,
            bytes_accessed=12 * col_count * depth,
            transcendentals=0,
        ),
    )(image[0], measured[0], row_weight, col_weight, band_weight, band_shift)
    return updated[None]


def solution(mesh):
    return jax.shard_map(
        functools.partial(per_device, mesh.shape["blk"], mesh.shape["gy"]),
        mesh=mesh,
        in_specs=(
            P(None, "blk", "gy"),
            P(None, "blk", None),
            P("blk", None),
            P("blk", "gy"),
            P("blk", "gy", None),
            P(),
        ),
        out_specs=P(None, "blk", "gy"),
        check_vma=False,
    )
```

```python
import functools

import jax
import jax.numpy as jnp
from jax import lax
from jax.experimental import pallas as pl
from jax.experimental.pallas import tpu as pltpu
from jax.sharding import PartitionSpec as P

PW = 128
SMOOTH = 0.25
SHIFTS = 4
MESH = pl.DeviceIdType.MESH


def roll_lanes(rows, amount):
    return pltpu.roll(rows, amount % rows.shape[1], 1)


def diagonal_sum(product):
    parts = [product[c : c + PW] for c in range(0, product.shape[0], PW)]
    rows = jnp.concatenate(parts + [jnp.zeros((PW, PW), jnp.float32)], axis=1)
    half = PW // 2
    while half >= 8:
        rows = rows[:half] + roll_lanes(rows[half:], half)
        half //= 2
    sub = lax.broadcasted_iota(jnp.int32, rows.shape, 0)
    for level in (4, 2, 1):
        rows = jnp.where(sub & level != 0, roll_lanes(rows, level), rows)
    return jnp.sum(rows, axis=0, keepdims=True)


def band_rows(line, col_count):
    rows = jnp.broadcast_to(line, (8, line.shape[1]))
    sub = lax.broadcasted_iota(jnp.int32, rows.shape, 0)
    for level in (4, 2, 1):
        rows = jnp.where(sub & level != 0, roll_lanes(rows, -level), rows)
    while rows.shape[0] < PW:
        rows = jnp.concatenate([rows, roll_lanes(rows, -rows.shape[0])], axis=0)
    return jnp.concatenate([rows[:, c : c + PW] for c in range(0, col_count, PW)], axis=0)


def kernel(
    blocks, groups,
    image_hbm, measured_hbm, row_hbm, col_hbm, band_ref, shift_ref, out_ref,
    image_ref, measured_ref, row_ref, col_ref, weights, copies, shift_rows, placed, footprints, partial, cut, panels, edge_out, edge_in,
    up_sem, down_sem, side_sem, weight_sem,
    foot_send, foot_recv, part_send, part_recv, cut_send, cut_recv, edge_send, edge_recv,
    load_sem,
):
    blk, gy = lax.axis_index("blk"), lax.axis_index("gy")
    line = blocks // 2
    spot, side = blk // 2, blk % 2
    local_tilts, depth, band_width = band_ref.shape
    col_count = image_hbm.shape[0]
    detector_len = measured_ref.shape[1]
    per_slab = col_count // PW
    window_panels = per_slab + 1
    reach = window_panels + SHIFTS - 1

    loads = [
        pltpu.make_async_copy(source, target, load_sem.at[number])
        for number, (source, target) in enumerate(
            [
                (image_hbm, image_ref),
                (band_ref, weights.at[blk]),
                (measured_hbm, measured_ref),
                (row_hbm, row_ref),
                (col_hbm, col_ref),
            ]
        )
    ]
    for load in loads:
        load.start()
    edge_in[...] = jnp.zeros_like(edge_in)
    barrier = pltpu.get_barrier_semaphore()

    def greet_blk(step, carry):
        peer = lax.rem(blk + step, blocks)
        pl.semaphore_signal(barrier, inc=1, device_id=(peer, gy), device_id_type=MESH)
        return carry

    def greet_gy(step, carry):
        peer = lax.rem(gy + step, groups)
        pl.semaphore_signal(barrier, inc=1, device_id=(blk, peer), device_id_type=MESH)
        return carry

    lax.fori_loop(1, blocks, greet_blk, 0)
    lax.fori_loop(1, groups, greet_gy, 0)
    pl.semaphore_wait(barrier, blocks + groups - 2)

    def send_weights(block, tilt, sems, to, source):
        held = weights.at[block, tilt]
        return pltpu.make_async_remote_copy(
            src_ref=held if source is None else source.at[tilt], dst_ref=held,
            send_sem=sems.at[block, tilt], recv_sem=weight_sem.at[block, tilt],
            device_id=(to, gy), device_id_type=MESH,
        )

    def send_up(block, tilt, source=None):
        return send_weights(block, tilt, up_sem, lax.rem(blk + 2, blocks), source)

    def send_down(block, tilt, source=None):
        return send_weights(block, tilt, down_sem, lax.rem(blk + blocks - 2, blocks), source)

    def send_side(block, tilt, source=None):
        return send_weights(block, tilt, side_sem, blk + 1 - 2 * side, source)

    def send_foot(block):
        return pltpu.make_async_remote_copy(
            src_ref=placed.at[block], dst_ref=footprints.at[blk],
            send_sem=foot_send.at[block], recv_sem=foot_recv.at[blk],
            device_id=(block, gy), device_id_type=MESH,
        )

    def foot_from(block):
        return pltpu.make_async_remote_copy(
            src_ref=placed.at[block], dst_ref=footprints.at[block],
            send_sem=foot_send.at[block], recv_sem=foot_recv.at[block],
            device_id=(block, gy), device_id_type=MESH,
        )

    def edge_copy(which, to):
        return pltpu.make_async_remote_copy(
            src_ref=edge_out.at[which], dst_ref=edge_in.at[which, pl.ds(0, 8)],
            send_sem=edge_send.at[which], recv_sem=edge_recv.at[which],
            device_id=(blk, to), device_id_type=MESH,
        )

    def tail_copy():
        return edge_copy(0, lax.rem(gy + 1, groups))

    def head_copy():
        return edge_copy(1, lax.rem(gy + groups - 1, groups))

    last = local_tilts - 1
    can_up, can_down = spot < line - 1, spot > 0
    for tilt in range(local_tilts):

        @pl.when(can_up)
        def _():
            send_up(blk, tilt, band_ref).start()

        @pl.when(can_down)
        def _():
            send_down(blk, tilt, band_ref).start()

        send_side(blk, tilt, band_ref).start()

    loads[0].wait()
    copies[...] = image_ref[...].astype(jnp.bfloat16)
    slab = lax.broadcasted_iota(jnp.int32, shift_ref.shape, 0)
    own_shift = jnp.sum(jnp.where(slab == blk, shift_ref[...], 0), axis=0, keepdims=True)
    square = (blocks * local_tilts, blocks * local_tilts)
    diagonal = lax.broadcasted_iota(jnp.int32, square, 0) == lax.broadcasted_iota(
        jnp.int32, square, 1
    )
    own_shift = jnp.where(diagonal, jnp.broadcast_to(own_shift, square), 0)
    own_shift = jnp.sum(own_shift, axis=1, keepdims=True)
    shift_rows[...] = jnp.broadcast_to(own_shift, shift_rows.shape)

    edge_out[0] = image_ref[:, depth - PW :].T[PW - 8 :]
    edge_out[1] = image_ref[:, :PW].T[:8]

    @pl.when(gy < groups - 1)
    def _():
        tail_copy().start()

    @pl.when(gy > 0)
    def _():
        head_copy().start()

    def wide(block):
        return jnp.concatenate([weights[block, t] for t in range(local_tilts)], axis=1)

    def project(block, tilt):
        product = jnp.dot(
            copies[...], weights[block, tilt], preferred_element_type=jnp.float32
        )
        window = diagonal_sum(product)
        shift = shift_rows[pl.ds(block * local_tilts + tilt, 1), :]
        for panel in range(reach):
            total = jnp.zeros((1, PW), jnp.float32)
            for k in range(SHIFTS):
                if 0 <= panel - k < window_panels:
                    piece = window[:, (panel - k) * PW : (panel - k + 1) * PW]
                    total = jnp.where(shift == k, piece, total)
            placed[block, pl.ds(tilt, 1), pl.ds(panel * PW, PW)] = total
        if tilt < last:
            return

        @pl.when(block != blk)
        def _():
            send_foot(block).start()

        @pl.when(block == blk)
        def _():
            footprints[blk] = placed[blk]

    partner = blk + 1 - 2 * side
    handover = max(line - 1, 2)

    def gather_step(step, carry):
        below, above = spot - step, spot + step

        @pl.when((step == handover) & can_up)
        def _():
            send_up(partner, last).start()

        @pl.when((step == handover) & can_down)
        def _():
            send_down(partner, last).start()

        for tilt in range(local_tilts):
            across = (step > 1) | (tilt < last)

            @pl.when((step > 0) & (below >= 0))
            def _():
                block = below * 2 + side
                send_up(block, tilt).wait_recv()

                @pl.when(can_up)
                def _():
                    send_up(block, tilt).start()

                @pl.when(across)
                def _():
                    send_side(block, tilt).start()

            @pl.when((step > 0) & (above < line))
            def _():
                block = above * 2 + side
                send_down(block, tilt).wait_recv()

                @pl.when(can_down)
                def _():
                    send_down(block, tilt).start()

                @pl.when(across)
                def _():
                    send_side(block, tilt).start()

        def visit(turn, carry):
            kind = turn // 2
            far = jnp.where(kind == 2, 1, step - kind)
            place = jnp.where(turn % 2 == 0, spot - far, spot + far)
            inside = (far >= 0) & (place >= 0) & (place < line) & ((far > 0) | (turn % 2 == 0))
            inside = inside & ((kind < 2) | (step == line))
            block = place * 2 + jnp.where(kind == 0, side, 1 - side)
            late = (kind == 1) & (far == 1)
            for tilt in range(local_tilts):
                wanted = ~late & (kind < 2) if tilt == last else kind < 2
                wanted = wanted | (kind == 2) if tilt == last else wanted

                @pl.when(inside & wanted)
                def _():
                    @pl.when(kind > 0)
                    def _():
                        send_side(block, tilt).wait_recv()

                    project(block, tilt)

            return carry

        return lax.fori_loop(0, 6, visit, carry)

    loads[1].wait()
    lax.fori_loop(0, line + 1, gather_step, 0)

    def take_foot(step, carry):
        foot_from(lax.rem(blk + step, blocks)).wait_recv()
        return carry

    lax.fori_loop(1, blocks, take_foot, 0)

    partial[gy] = jnp.zeros((local_tilts, detector_len), jnp.float32)
    for source in range(blocks):
        bins = pl.ds(source * per_slab * PW, reach * PW)
        partial[gy, :, bins] = partial[gy, :, bins] + footprints[source]

    def part_copy(to, slot):
        return pltpu.make_async_remote_copy(
            src_ref=partial.at[gy], dst_ref=partial.at[slot],
            send_sem=part_send.at[to], recv_sem=part_recv.at[slot],
            device_id=(blk, to), device_id_type=MESH,
        )

    def give_part(step, carry):
        part_copy(lax.rem(gy + step, groups), gy).start()
        return carry

    def take_part(step, carry):
        peer = lax.rem(gy + step, groups)
        part_copy(peer, peer).wait_recv()
        return carry

    lax.fori_loop(1, groups, give_part, 0)
    lax.fori_loop(1, groups, take_part, 0)

    loads[2].wait()
    loads[3].wait()
    projection = partial[0]
    for group in range(1, groups):
        projection = projection + partial[group]
    weighted = (row_ref[...] * (measured_ref[...] - projection)).astype(jnp.bfloat16)
    weighted = weighted.astype(jnp.float32)
    for block in range(blocks):
        start = block * per_slab * PW
        cut[block] = weighted[:, start : start + reach * PW]

    def cut_copy(to, slot):
        return pltpu.make_async_remote_copy(
            src_ref=cut.at[to], dst_ref=panels.at[slot],
            send_sem=cut_send.at[to], recv_sem=cut_recv.at[slot],
            device_id=(to, gy), device_id_type=MESH,
        )

    def give_cut(step, carry):
        cut_copy(lax.rem(blk + step, blocks), blk).start()
        return carry

    lax.fori_loop(1, blocks, give_cut, 0)
    panels[blk] = cut[blk]
    out_ref[...] = jnp.zeros_like(out_ref)

    def back_step(step, carry):
        source = lax.rem(blk + step, blocks)

        @pl.when(step > 0)
        def _():
            cut_copy(source, source).wait_recv()

        sheared = []
        for t in range(local_tilts):
            shift = shift_rows[pl.ds(source * local_tilts + t, 1), :]
            pieces = []
            for panel in range(window_panels):
                piece = panels[source, pl.ds(t, 1), pl.ds(panel * PW, PW)]
                for k in range(1, SHIFTS):
                    moved = panels[source, pl.ds(t, 1), pl.ds((panel + k) * PW, PW)]
                    piece = jnp.where(shift == k, moved, piece)
                pieces.append(piece)
            sheared.append(band_rows(jnp.concatenate(pieces, axis=1), col_count))
        rows = jnp.concatenate(sheared, axis=1).astype(jnp.bfloat16)
        out_ref[...] += lax.dot_general(
            rows, wide(source), (((1,), (1,)), ((), ())), preferred_element_type=jnp.float32
        )
        return carry

    lax.fori_loop(0, blocks, back_step, 0)

    @pl.when(gy > 0)
    def _():
        tail_copy().wait_recv()

    @pl.when(gy < groups - 1)
    def _():
        head_copy().wait_recv()

    loads[4].wait()
    before = edge_in[0].T[:, 7:8]
    after = edge_in[1].T[:, 0:1]
    chunk = 32
    lane = lax.broadcasted_iota(jnp.int32, (chunk, depth), 1)
    for top in range(0, col_count, chunk):
        rows = slice(top, top + chunk)
        here = image_ref[rows, :]
        left = jnp.where(lane == 0, before[rows], roll_lanes(here, 1))
        right = jnp.where(lane == depth - 1, after[rows], roll_lanes(here, -1))
        out_ref[rows, :] = (
            here + col_ref[rows, :] * out_ref[rows, :] + SMOOTH * (left + right - 2.0 * here)
        )

    @pl.when(gy < groups - 1)
    def _():
        tail_copy().wait_send()

    @pl.when(gy > 0)
    def _():
        head_copy().wait_send()

    def settle_line(place, carry):
        block = place * 2 + side
        for tilt in range(local_tilts):

            @pl.when((place <= spot) & can_up)
            def _():
                send_up(block, tilt).wait_send()

            @pl.when((place >= spot) & can_down)
            def _():
                send_down(block, tilt).wait_send()

            near = (place == spot - 1) | (place == spot + 1)

            @pl.when(~near | (tilt < last))
            def _():
                send_side(block, tilt).wait_send()

        return carry

    @pl.when(can_up)
    def _():
        send_up(partner, last).wait_send()

    @pl.when(can_down)
    def _():
        send_down(partner, last).wait_send()

    def settle_blk(step, carry):
        peer = lax.rem(blk + step, blocks)
        send_foot(peer).wait_send()
        cut_copy(peer, blk).wait_send()
        return carry

    def settle_gy(step, carry):
        part_copy(lax.rem(gy + step, groups), gy).wait_send()
        return carry

    lax.fori_loop(0, line, settle_line, 0)
    lax.fori_loop(1, blocks, settle_blk, 0)
    lax.fori_loop(1, groups, settle_gy, 0)


def per_device(blocks, groups, image, measured, row_weight, col_weight, band_weight, band_shift):
    _, col_count, depth = image.shape
    local_tilts, _, band_width = band_weight.shape
    detector_len = measured.shape[2]
    reach = (col_count // PW + SHIFTS) * PW
    window = (blocks, local_tilts, reach)
    dma = pltpu.SemaphoreType.DMA
    units = dma((blocks, local_tilts))
    updated = pl.pallas_call(
        functools.partial(kernel, blocks, groups),
        out_shape=jax.ShapeDtypeStruct((col_count, depth), jnp.float32),
        in_specs=[pl.BlockSpec(memory_space=pl.ANY)] * 5
        + [pl.BlockSpec(memory_space=pltpu.VMEM)],
        out_specs=pl.BlockSpec(memory_space=pltpu.VMEM),
        scratch_shapes=[
            pltpu.VMEM((col_count, depth), jnp.float32),
            pltpu.VMEM((local_tilts, detector_len), jnp.float32),
            pltpu.VMEM((local_tilts, detector_len), jnp.float32),
            pltpu.VMEM((col_count, depth), jnp.float32),
            pltpu.VMEM((blocks,) + band_weight.shape, jnp.bfloat16),
            pltpu.VMEM((col_count, depth), jnp.bfloat16),
            pltpu.VMEM((blocks * local_tilts, PW), jnp.int32),
            pltpu.VMEM(window, jnp.float32),
            pltpu.VMEM(window, jnp.float32),
            pltpu.VMEM((groups, local_tilts, detector_len), jnp.float32),
            pltpu.VMEM(window, jnp.float32),
            pltpu.VMEM(window, jnp.float32),
            pltpu.VMEM((2, 8, col_count), jnp.float32),
            pltpu.VMEM((2, PW, col_count), jnp.float32),
            units, units, units, units,
            dma((blocks,)), dma((blocks,)), dma((groups,)), dma((groups,)),
            dma((blocks,)), dma((blocks,)), dma((2,)), dma((2,)), dma((5,)),
        ],
        compiler_params=pltpu.CompilerParams(
            collective_id=0, has_side_effects=True, vmem_limit_bytes=56 * 1024 * 1024
        ),
        cost_estimate=pl.CostEstimate(
            flops=4 * blocks * local_tilts * band_width * col_count * depth,
            bytes_accessed=12 * col_count * depth,
            transcendentals=0,
        ),
    )(image[0], measured[0], row_weight, col_weight, band_weight, band_shift.T)
    return updated[None]


def solution(mesh):
    return jax.shard_map(
        functools.partial(per_device, mesh.shape["blk"], mesh.shape["gy"]),
        mesh=mesh,
        in_specs=(
            P(None, "blk", "gy"),
            P(None, "blk", None),
            P("blk", None),
            P("blk", "gy"),
            P("blk", "gy", None),
            P(),
        ),
        out_specs=P(None, "blk", "gy"),
        check_vma=False,
    )
```

```python
import functools

import jax
import jax.numpy as jnp
from jax import lax
from jax.experimental import pallas as pl
from jax.experimental.pallas import tpu as pltpu
from jax.sharding import PartitionSpec as P

PW = 128
SMOOTH = 0.25
SHIFTS = 4
MESH = pl.DeviceIdType.MESH


def roll_lanes(rows, amount):
    return pltpu.roll(rows, amount % rows.shape[1], 1)


def diagonal_sum(product):
    parts = [product[c : c + PW] for c in range(0, product.shape[0], PW)]
    rows = jnp.concatenate(parts + [jnp.zeros((PW, PW), jnp.float32)], axis=1)
    half = PW // 2
    while half >= 8:
        rows = rows[:half] + roll_lanes(rows[half:], half)
        half //= 2
    sub = lax.broadcasted_iota(jnp.int32, rows.shape, 0)
    for level in (4, 2, 1):
        rows = jnp.where(sub & level != 0, roll_lanes(rows, level), rows)
    return jnp.sum(rows, axis=0, keepdims=True)


def band_rows(line, col_count):
    rows = jnp.broadcast_to(line, (8, line.shape[1]))
    sub = lax.broadcasted_iota(jnp.int32, rows.shape, 0)
    for level in (4, 2, 1):
        rows = jnp.where(sub & level != 0, roll_lanes(rows, -level), rows)
    while rows.shape[0] < PW:
        rows = jnp.concatenate([rows, roll_lanes(rows, -rows.shape[0])], axis=0)
    return jnp.concatenate([rows[:, c : c + PW] for c in range(0, col_count, PW)], axis=0)


def kernel(
    blocks, groups,
    image_hbm, measured_hbm, row_hbm, col_hbm, band_ref, shift_ref, out_ref,
    image_ref, measured_ref, row_ref, col_ref, weights, copies, shift_rows, placed, footprints, partial, cut, panels, edge_out, edge_in,
    up_sem, down_sem, side_sem, weight_sem,
    foot_send, foot_recv, part_send, part_recv, cut_send, cut_recv, edge_send, edge_recv,
    load_sem,
):
    blk, gy = lax.axis_index("blk"), lax.axis_index("gy")
    line = blocks // 2
    spot, side = blk // 2, blk % 2
    local_tilts, depth, band_width = band_ref.shape
    col_count = image_hbm.shape[0]
    detector_len = measured_ref.shape[1]
    per_slab = col_count // PW
    window_panels = per_slab + 1
    reach = window_panels + SHIFTS - 1

    loads = [
        pltpu.make_async_copy(source, target, load_sem.at[number])
        for number, (source, target) in enumerate(
            [
                (image_hbm, image_ref),
                (band_ref, weights.at[blk]),
                (measured_hbm, measured_ref),
                (row_hbm, row_ref),
                (col_hbm, col_ref),
            ]
        )
    ]
    for load in loads:
        load.start()
    edge_in[...] = jnp.zeros_like(edge_in)
    barrier = pltpu.get_barrier_semaphore()

    def greet_blk(step, carry):
        peer = lax.rem(blk + step, blocks)
        pl.semaphore_signal(barrier, inc=1, device_id=(peer, gy), device_id_type=MESH)
        return carry

    def greet_gy(step, carry):
        peer = lax.rem(gy + step, groups)
        pl.semaphore_signal(barrier, inc=1, device_id=(blk, peer), device_id_type=MESH)
        return carry

    lax.fori_loop(1, blocks, greet_blk, 0)
    lax.fori_loop(1, groups, greet_gy, 0)
    pl.semaphore_wait(barrier, blocks + groups - 2)

    def send_weights(block, tilt, sems, to, source):
        held = weights.at[block, tilt]
        return pltpu.make_async_remote_copy(
            src_ref=held if source is None else source.at[tilt], dst_ref=held,
            send_sem=sems.at[block, tilt], recv_sem=weight_sem.at[block, tilt],
            device_id=(to, gy), device_id_type=MESH,
        )

    def send_up(block, tilt, source=None):
        return send_weights(block, tilt, up_sem, lax.rem(blk + 2, blocks), source)

    def send_down(block, tilt, source=None):
        return send_weights(block, tilt, down_sem, lax.rem(blk + blocks - 2, blocks), source)

    def send_side(block, tilt, source=None):
        return send_weights(block, tilt, side_sem, blk + 1 - 2 * side, source)

    def send_foot(block):
        return pltpu.make_async_remote_copy(
            src_ref=placed.at[block], dst_ref=footprints.at[blk],
            send_sem=foot_send.at[block], recv_sem=foot_recv.at[blk],
            device_id=(block, gy), device_id_type=MESH,
        )

    def foot_from(block):
        return pltpu.make_async_remote_copy(
            src_ref=placed.at[block], dst_ref=footprints.at[block],
            send_sem=foot_send.at[block], recv_sem=foot_recv.at[block],
            device_id=(block, gy), device_id_type=MESH,
        )

    def edge_copy(which, to):
        return pltpu.make_async_remote_copy(
            src_ref=edge_out.at[which], dst_ref=edge_in.at[which, pl.ds(0, 8)],
            send_sem=edge_send.at[which], recv_sem=edge_recv.at[which],
            device_id=(blk, to), device_id_type=MESH,
        )

    def tail_copy():
        return edge_copy(0, lax.rem(gy + 1, groups))

    def head_copy():
        return edge_copy(1, lax.rem(gy + groups - 1, groups))

    last = local_tilts - 1
    can_up, can_down = spot < line - 1, spot > 0
    for tilt in range(local_tilts):

        @pl.when(can_up)
        def _():
            send_up(blk, tilt, band_ref).start()

        @pl.when(can_down)
        def _():
            send_down(blk, tilt, band_ref).start()

        send_side(blk, tilt, band_ref).start()

    loads[0].wait()
    copies[...] = image_ref[...].astype(jnp.bfloat16)
    slab = lax.broadcasted_iota(jnp.int32, shift_ref.shape, 0)
    own_shift = jnp.sum(jnp.where(slab == blk, shift_ref[...], 0), axis=0, keepdims=True)
    square = (blocks * local_tilts, blocks * local_tilts)
    diagonal = lax.broadcasted_iota(jnp.int32, square, 0) == lax.broadcasted_iota(
        jnp.int32, square, 1
    )
    own_shift = jnp.where(diagonal, jnp.broadcast_to(own_shift, square), 0)
    own_shift = jnp.sum(own_shift, axis=1, keepdims=True)
    shift_rows[...] = jnp.broadcast_to(own_shift, shift_rows.shape)

    edge_out[0] = image_ref[:, depth - PW :].T[PW - 8 :]
    edge_out[1] = image_ref[:, :PW].T[:8]

    @pl.when(gy < groups - 1)
    def _():
        tail_copy().start()

    @pl.when(gy > 0)
    def _():
        head_copy().start()

    def wide(block):
        return jnp.concatenate([weights[block, t] for t in range(local_tilts)], axis=1)

    def project(block, tilt):
        product = jnp.dot(
            copies[...], weights[block, tilt], preferred_element_type=jnp.float32
        )
        window = diagonal_sum(product)
        shift = shift_rows[pl.ds(block * local_tilts + tilt, 1), :]
        for panel in range(reach):
            total = jnp.zeros((1, PW), jnp.float32)
            for k in range(SHIFTS):
                if 0 <= panel - k < window_panels:
                    piece = window[:, (panel - k) * PW : (panel - k + 1) * PW]
                    total = jnp.where(shift == k, piece, total)
            placed[block, pl.ds(tilt, 1), pl.ds(panel * PW, PW)] = total
        if tilt < last:
            return

        @pl.when(block != blk)
        def _():
            send_foot(block).start()

        @pl.when(block == blk)
        def _():
            footprints[blk] = placed[blk]

    partner = blk + 1 - 2 * side
    handover = max(line - 1, 2)

    def gather_step(step, carry):
        below, above = spot - step, spot + step

        @pl.when((step == handover) & can_up)
        def _():
            send_up(partner, last).start()

        @pl.when((step == handover) & can_down)
        def _():
            send_down(partner, last).start()

        for tilt in range(local_tilts):
            across = (step > 1) | (tilt < last)

            @pl.when((step > 0) & (below >= 0))
            def _():
                block = below * 2 + side
                send_up(block, tilt).wait_recv()

                @pl.when(can_up)
                def _():
                    send_up(block, tilt).start()

                @pl.when(across)
                def _():
                    send_side(block, tilt).start()

            @pl.when((step > 0) & (above < line))
            def _():
                block = above * 2 + side
                send_down(block, tilt).wait_recv()

                @pl.when(can_down)
                def _():
                    send_down(block, tilt).start()

                @pl.when(across)
                def _():
                    send_side(block, tilt).start()

        def visit(turn, carry):
            kind = turn // 2
            far = jnp.where(kind == 2, 1, step - kind)
            place = jnp.where(turn % 2 == 0, spot - far, spot + far)
            inside = (far >= 0) & (place >= 0) & (place < line) & ((far > 0) | (turn % 2 == 0))
            inside = inside & ((kind < 2) | (step == line))
            block = place * 2 + jnp.where(kind == 0, side, 1 - side)
            late = (kind == 1) & (far == 1)
            for tilt in range(local_tilts):
                wanted = ~late & (kind < 2) if tilt == last else kind < 2
                wanted = wanted | (kind == 2) if tilt == last else wanted

                @pl.when(inside & wanted)
                def _():
                    @pl.when(kind > 0)
                    def _():
                        send_side(block, tilt).wait_recv()

                    project(block, tilt)

            return carry

        return lax.fori_loop(0, 6, visit, carry)

    loads[1].wait()
    lax.fori_loop(0, line + 1, gather_step, 0)

    def take_foot(step, carry):
        foot_from(lax.rem(blk + step, blocks)).wait_recv()
        return carry

    lax.fori_loop(1, blocks, take_foot, 0)

    partial[gy] = jnp.zeros((local_tilts, detector_len), jnp.float32)
    for source in range(blocks):
        bins = pl.ds(source * per_slab * PW, reach * PW)
        partial[gy, :, bins] = partial[gy, :, bins] + footprints[source]

    def part_copy(to, slot):
        return pltpu.make_async_remote_copy(
            src_ref=partial.at[gy], dst_ref=partial.at[slot],
            send_sem=part_send.at[to], recv_sem=part_recv.at[slot],
            device_id=(blk, to), device_id_type=MESH,
        )

    def give_part(step, carry):
        part_copy(lax.rem(gy + step, groups), gy).start()
        return carry

    def take_part(step, carry):
        peer = lax.rem(gy + step, groups)
        part_copy(peer, peer).wait_recv()
        return carry

    lax.fori_loop(1, groups, give_part, 0)
    lax.fori_loop(1, groups, take_part, 0)

    loads[2].wait()
    loads[3].wait()
    projection = partial[0]
    for group in range(1, groups):
        projection = projection + partial[group]
    weighted = (row_ref[...] * (measured_ref[...] - projection)).astype(jnp.bfloat16)
    weighted = weighted.astype(jnp.float32)
    for block in range(blocks):
        start = block * per_slab * PW
        cut[block] = weighted[:, start : start + reach * PW]

    def cut_copy(to, slot):
        return pltpu.make_async_remote_copy(
            src_ref=cut.at[to], dst_ref=panels.at[slot],
            send_sem=cut_send.at[to], recv_sem=cut_recv.at[slot],
            device_id=(to, gy), device_id_type=MESH,
        )

    def give_cut(step, carry):
        cut_copy(lax.rem(blk + step, blocks), blk).start()
        return carry

    lax.fori_loop(1, blocks, give_cut, 0)
    panels[blk] = cut[blk]
    out_ref[...] = jnp.zeros_like(out_ref)

    def back_step(step, carry):
        source = lax.rem(blk + step, blocks)

        @pl.when(step > 0)
        def _():
            cut_copy(source, source).wait_recv()

        sheared = []
        for t in range(local_tilts):
            shift = shift_rows[pl.ds(source * local_tilts + t, 1), :]
            pieces = []
            for panel in range(window_panels):
                piece = panels[source, pl.ds(t, 1), pl.ds(panel * PW, PW)]
                for k in range(1, SHIFTS):
                    moved = panels[source, pl.ds(t, 1), pl.ds((panel + k) * PW, PW)]
                    piece = jnp.where(shift == k, moved, piece)
                pieces.append(piece)
            sheared.append(band_rows(jnp.concatenate(pieces, axis=1), col_count))
        rows = jnp.concatenate(sheared, axis=1).astype(jnp.bfloat16)
        out_ref[...] += lax.dot_general(
            rows, wide(source), (((1,), (1,)), ((), ())), preferred_element_type=jnp.float32
        )
        return carry

    lax.fori_loop(0, blocks, back_step, 0)

    @pl.when(gy > 0)
    def _():
        tail_copy().wait_recv()

    @pl.when(gy < groups - 1)
    def _():
        head_copy().wait_recv()

    loads[4].wait()
    before = edge_in[0].T[:, 7:8]
    after = edge_in[1].T[:, 0:1]
    chunk = 32
    lane = lax.broadcasted_iota(jnp.int32, (chunk, depth), 1)
    for top in range(0, col_count, chunk):
        rows = slice(top, top + chunk)
        here = image_ref[rows, :]
        left = jnp.where(lane == 0, before[rows], roll_lanes(here, 1))
        right = jnp.where(lane == depth - 1, after[rows], roll_lanes(here, -1))
        out_ref[rows, :] = (
            here + col_ref[rows, :] * out_ref[rows, :] + SMOOTH * (left + right - 2.0 * here)
        )

    @pl.when(gy < groups - 1)
    def _():
        tail_copy().wait_send()

    @pl.when(gy > 0)
    def _():
        head_copy().wait_send()

    def settle_line(place, carry):
        block = place * 2 + side
        for tilt in range(local_tilts):

            @pl.when((place <= spot) & can_up)
            def _():
                send_up(block, tilt).wait_send()

            @pl.when((place >= spot) & can_down)
            def _():
                send_down(block, tilt).wait_send()

            near = (place == spot - 1) | (place == spot + 1)

            @pl.when(~near | (tilt < last))
            def _():
                send_side(block, tilt).wait_send()

        return carry

    @pl.when(can_up)
    def _():
        send_up(partner, last).wait_send()

    @pl.when(can_down)
    def _():
        send_down(partner, last).wait_send()

    def settle_blk(step, carry):
        peer = lax.rem(blk + step, blocks)
        send_foot(peer).wait_send()
        cut_copy(peer, blk).wait_send()
        return carry

    def settle_gy(step, carry):
        part_copy(lax.rem(gy + step, groups), gy).wait_send()
        return carry

    lax.fori_loop(0, line, settle_line, 0)
    lax.fori_loop(1, blocks, settle_blk, 0)
    lax.fori_loop(1, groups, settle_gy, 0)


def per_device(blocks, groups, image, measured, row_weight, col_weight, band_weight, band_shift):
    _, col_count, depth = image.shape
    local_tilts, _, band_width = band_weight.shape
    detector_len = measured.shape[2]
    reach = (col_count // PW + SHIFTS) * PW
    window = (blocks, local_tilts, reach)
    dma = pltpu.SemaphoreType.DMA
    units = dma((blocks, local_tilts))
    updated = pl.pallas_call(
        functools.partial(kernel, blocks, groups),
        out_shape=pltpu.VMEM((col_count, depth), jnp.float32),
        in_specs=[pl.BlockSpec(memory_space=pl.ANY)] * 5
        + [pl.BlockSpec(memory_space=pltpu.VMEM)],
        out_specs=pl.BlockSpec(memory_space=pltpu.VMEM),
        scratch_shapes=[
            pltpu.VMEM((col_count, depth), jnp.float32),
            pltpu.VMEM((local_tilts, detector_len), jnp.float32),
            pltpu.VMEM((local_tilts, detector_len), jnp.float32),
            pltpu.VMEM((col_count, depth), jnp.float32),
            pltpu.VMEM((blocks,) + band_weight.shape, jnp.bfloat16),
            pltpu.VMEM((col_count, depth), jnp.bfloat16),
            pltpu.VMEM((blocks * local_tilts, PW), jnp.int32),
            pltpu.VMEM(window, jnp.float32),
            pltpu.VMEM(window, jnp.float32),
            pltpu.VMEM((groups, local_tilts, detector_len), jnp.float32),
            pltpu.VMEM(window, jnp.float32),
            pltpu.VMEM(window, jnp.float32),
            pltpu.VMEM((2, 8, col_count), jnp.float32),
            pltpu.VMEM((2, PW, col_count), jnp.float32),
            units, units, units, units,
            dma((blocks,)), dma((blocks,)), dma((groups,)), dma((groups,)),
            dma((blocks,)), dma((blocks,)), dma((2,)), dma((2,)), dma((5,)),
        ],
        compiler_params=pltpu.CompilerParams(
            collective_id=0, has_side_effects=True, vmem_limit_bytes=56 * 1024 * 1024
        ),
        cost_estimate=pl.CostEstimate(
            flops=4 * blocks * local_tilts * band_width * col_count * depth,
            bytes_accessed=12 * col_count * depth,
            transcendentals=0,
        ),
    )(image[0], measured[0], row_weight, col_weight, band_weight, band_shift.T)
    return updated[None]


def solution(mesh):
    return jax.shard_map(
        functools.partial(per_device, mesh.shape["blk"], mesh.shape["gy"]),
        mesh=mesh,
        in_specs=(
            P(None, "blk", "gy"),
            P(None, "blk", None),
            P("blk", None),
            P("blk", "gy"),
            P("blk", "gy", None),
            P(),
        ),
        out_specs=P(None, "blk", "gy"),
        check_vma=False,
    )
```

```python
import functools
import math

import jax
import jax.numpy as jnp
from jax import lax
from jax.experimental import pallas as pl
from jax.experimental.pallas import tpu as pltpu
from jax.sharding import PartitionSpec as P

PW = 128
SMOOTH = 0.25
SHIFTS = 4
MESH = pl.DeviceIdType.MESH


def roll_lanes(rows, amount):
    return pltpu.roll(rows, amount % rows.shape[1], 1)


def diagonal_sum(product):
    parts = [product[c : c + PW] for c in range(0, product.shape[0], PW)]
    rows = jnp.concatenate(parts + [jnp.zeros((PW, PW), jnp.float32)], axis=1)
    half = PW // 2
    while half >= 8:
        rows = rows[:half] + roll_lanes(rows[half:], half)
        half //= 2
    sub = lax.broadcasted_iota(jnp.int32, rows.shape, 0)
    for level in (4, 2, 1):
        rows = jnp.where(sub & level != 0, roll_lanes(rows, level), rows)
    return jnp.sum(rows, axis=0, keepdims=True)


def band_rows(line, col_count):
    rows = jnp.broadcast_to(line, (8, line.shape[1]))
    sub = lax.broadcasted_iota(jnp.int32, rows.shape, 0)
    for level in (4, 2, 1):
        rows = jnp.where(sub & level != 0, roll_lanes(rows, -level), rows)
    while rows.shape[0] < PW:
        rows = jnp.concatenate([rows, roll_lanes(rows, -rows.shape[0])], axis=0)
    return jnp.concatenate([rows[:, c : c + PW] for c in range(0, col_count, PW)], axis=0)


def kernel(
    blocks, groups,
    image_hbm, measured_hbm, row_hbm, col_hbm, band_ref, shift_ref, out_ref,
    image_ref, measured_ref, row_ref, col_ref, weights, wide, sheared, copies, shift_rows, placed, footprints, partial, cut, panels, edge_out, edge_in,
    up_sem, down_sem, side_sem, weight_sem,
    foot_send, foot_recv, part_send, part_recv, cut_send, cut_recv, edge_send, edge_recv,
    load_sem,
):
    blk, gy = lax.axis_index("blk"), lax.axis_index("gy")
    line = blocks // 2
    spot, side = blk // 2, blk % 2
    local_tilts, depth, band_width = band_ref.shape
    col_count = image_hbm.shape[0]
    detector_len = measured_ref.shape[1]
    per_slab = col_count // PW
    window_panels = per_slab + 1
    reach = window_panels + SHIFTS - 1

    loads = [
        pltpu.make_async_copy(source, target, load_sem.at[number])
        for number, (source, target) in enumerate(
            [
                (image_hbm, image_ref),
                (band_ref, weights.at[blk]),
                (measured_hbm, measured_ref),
                (row_hbm, row_ref),
                (col_hbm, col_ref),
            ]
        )
    ]
    for load in loads:
        load.start()
    edge_in[...] = jnp.zeros_like(edge_in)
    barrier = pltpu.get_barrier_semaphore()

    def greet_blk(step, carry):
        peer = lax.rem(blk + step, blocks)
        pl.semaphore_signal(barrier, inc=1, device_id=(peer, gy), device_id_type=MESH)
        return carry

    def greet_gy(step, carry):
        peer = lax.rem(gy + step, groups)
        pl.semaphore_signal(barrier, inc=1, device_id=(blk, peer), device_id_type=MESH)
        return carry

    lax.fori_loop(1, blocks, greet_blk, 0)
    lax.fori_loop(1, groups, greet_gy, 0)
    pl.semaphore_wait(barrier, blocks + groups - 2)

    def send_weights(block, tilt, sems, to, source):
        held = weights.at[block, tilt]
        return pltpu.make_async_remote_copy(
            src_ref=held if source is None else source.at[tilt], dst_ref=held,
            send_sem=sems.at[block, tilt], recv_sem=weight_sem.at[block, tilt],
            device_id=(to, gy), device_id_type=MESH,
        )

    def send_up(block, tilt, source=None):
        return send_weights(block, tilt, up_sem, lax.rem(blk + 2, blocks), source)

    def send_down(block, tilt, source=None):
        return send_weights(block, tilt, down_sem, lax.rem(blk + blocks - 2, blocks), source)

    def send_side(block, tilt, source=None):
        return send_weights(block, tilt, side_sem, blk + 1 - 2 * side, source)

    def send_foot(block):
        return pltpu.make_async_remote_copy(
            src_ref=placed.at[block], dst_ref=footprints.at[blk],
            send_sem=foot_send.at[block], recv_sem=foot_recv.at[blk],
            device_id=(block, gy), device_id_type=MESH,
        )

    def foot_from(block):
        return pltpu.make_async_remote_copy(
            src_ref=placed.at[block], dst_ref=footprints.at[block],
            send_sem=foot_send.at[block], recv_sem=foot_recv.at[block],
            device_id=(block, gy), device_id_type=MESH,
        )

    def edge_copy(which, to):
        return pltpu.make_async_remote_copy(
            src_ref=edge_out.at[which], dst_ref=edge_in.at[which, pl.ds(0, 8)],
            send_sem=edge_send.at[which], recv_sem=edge_recv.at[which],
            device_id=(blk, to), device_id_type=MESH,
        )

    def tail_copy():
        return edge_copy(0, lax.rem(gy + 1, groups))

    def head_copy():
        return edge_copy(1, lax.rem(gy + groups - 1, groups))

    last = local_tilts - 1
    can_up, can_down = spot < line - 1, spot > 0
    for tilt in range(local_tilts):

        @pl.when(can_up)
        def _():
            send_up(blk, tilt, band_ref).start()

        @pl.when(can_down)
        def _():
            send_down(blk, tilt, band_ref).start()

        send_side(blk, tilt, band_ref).start()

    loads[0].wait()
    copies[...] = image_ref[...].astype(jnp.bfloat16)
    slab = lax.broadcasted_iota(jnp.int32, shift_ref.shape, 0)
    own_shift = jnp.sum(jnp.where(slab == blk, shift_ref[...], 0), axis=0, keepdims=True)
    square = (blocks * local_tilts, blocks * local_tilts)
    diagonal = lax.broadcasted_iota(jnp.int32, square, 0) == lax.broadcasted_iota(
        jnp.int32, square, 1
    )
    own_shift = jnp.where(diagonal, jnp.broadcast_to(own_shift, square), 0)
    own_shift = jnp.sum(own_shift, axis=1, keepdims=True)
    shift_rows[...] = jnp.broadcast_to(own_shift, shift_rows.shape)

    edge_out[0] = image_ref[:, depth - PW :].T[PW - 8 :]
    edge_out[1] = image_ref[:, :PW].T[:8]

    @pl.when(gy < groups - 1)
    def _():
        tail_copy().start()

    @pl.when(gy > 0)
    def _():
        head_copy().start()

    def lanes_of(block, tilt):
        number = block * local_tilts + tilt
        return pl.ds(pl.multiple_of(number * band_width, band_width), band_width)

    def project(block, tilt):
        band = weights[block, tilt]
        wide[:, lanes_of(block, tilt)] = band
        product = jnp.dot(copies[...], band, preferred_element_type=jnp.float32)
        window = diagonal_sum(product)
        shift = shift_rows[pl.ds(block * local_tilts + tilt, 1), :]
        for panel in range(reach):
            total = jnp.zeros((1, PW), jnp.float32)
            for k in range(SHIFTS):
                if 0 <= panel - k < window_panels:
                    piece = window[:, (panel - k) * PW : (panel - k + 1) * PW]
                    total = jnp.where(shift == k, piece, total)
            placed[block, pl.ds(tilt, 1), pl.ds(panel * PW, PW)] = total
        if tilt < last:
            return

        @pl.when(block != blk)
        def _():
            send_foot(block).start()

        @pl.when(block == blk)
        def _():
            footprints[blk] = placed[blk]

    def smooth():
        @pl.when(gy > 0)
        def _():
            tail_copy().wait_recv()

        @pl.when(gy < groups - 1)
        def _():
            head_copy().wait_recv()

        before = edge_in[0].T[:, 7:8]
        after = edge_in[1].T[:, 0:1]
        chunk = 32
        lane = lax.broadcasted_iota(jnp.int32, (chunk, depth), 1)
        for top in range(0, col_count, chunk):
            rows = slice(top, top + chunk)
            here = image_ref[rows, :]
            left = jnp.where(lane == 0, before[rows], roll_lanes(here, 1))
            right = jnp.where(lane == depth - 1, after[rows], roll_lanes(here, -1))
            out_ref[rows, :] = here + SMOOTH * (left + right - 2.0 * here)

    partner = blk + 1 - 2 * side
    handover = max(line - 1, 2)

    def gather_step(step, carry):
        below, above = spot - step, spot + step

        @pl.when((step == handover) & can_up)
        def _():
            send_up(partner, last).start()

        @pl.when((step == handover) & can_down)
        def _():
            send_down(partner, last).start()

        for tilt in range(local_tilts):
            across = (step > 1) | (tilt < last)

            @pl.when((step > 0) & (below >= 0))
            def _():
                block = below * 2 + side
                send_up(block, tilt).wait_recv()

                @pl.when(can_up)
                def _():
                    send_up(block, tilt).start()

                @pl.when(across)
                def _():
                    send_side(block, tilt).start()

            @pl.when((step > 0) & (above < line))
            def _():
                block = above * 2 + side
                send_down(block, tilt).wait_recv()

                @pl.when(can_down)
                def _():
                    send_down(block, tilt).start()

                @pl.when(across)
                def _():
                    send_side(block, tilt).start()

        def visit(turn, carry):
            kind = turn // 2
            far = jnp.where(kind == 2, 1, step - kind)
            place = jnp.where(turn % 2 == 0, spot - far, spot + far)
            inside = (far >= 0) & (place >= 0) & (place < line) & ((far > 0) | (turn % 2 == 0))
            inside = inside & ((kind < 2) | (step == line))
            block = place * 2 + jnp.where(kind == 0, side, 1 - side)
            late = (kind == 1) & (far == 1)
            for tilt in range(local_tilts):
                wanted = ~late & (kind < 2) if tilt == last else kind < 2
                wanted = wanted | (kind == 2) if tilt == last else wanted

                @pl.when(inside & wanted)
                def _():
                    @pl.when(kind > 0)
                    def _():
                        send_side(block, tilt).wait_recv()

                    project(block, tilt)

            return carry

        lax.fori_loop(0, 6, visit, 0)

        @pl.when(step == line)
        def _():
            smooth()

        return carry

    loads[1].wait()
    lax.fori_loop(0, line + 1, gather_step, 0)

    def take_foot(step, carry):
        foot_from(lax.rem(blk + step, blocks)).wait_recv()
        return carry

    lax.fori_loop(1, blocks, take_foot, 0)

    partial[gy] = jnp.zeros((local_tilts, detector_len), jnp.float32)
    for source in range(blocks):
        bins = pl.ds(source * per_slab * PW, reach * PW)
        partial[gy, :, bins] = partial[gy, :, bins] + footprints[source]

    def part_copy(to, slot):
        return pltpu.make_async_remote_copy(
            src_ref=partial.at[gy], dst_ref=partial.at[slot],
            send_sem=part_send.at[to], recv_sem=part_recv.at[slot],
            device_id=(blk, to), device_id_type=MESH,
        )

    def give_part(step, carry):
        part_copy(lax.rem(gy + step, groups), gy).start()
        return carry

    def take_part(step, carry):
        peer = lax.rem(gy + step, groups)
        part_copy(peer, peer).wait_recv()
        return carry

    lax.fori_loop(1, groups, give_part, 0)
    lax.fori_loop(1, groups, take_part, 0)

    loads[2].wait()
    loads[3].wait()
    projection = partial[0]
    for group in range(1, groups):
        projection = projection + partial[group]
    weighted = (row_ref[...] * (measured_ref[...] - projection)).astype(jnp.bfloat16)
    weighted = weighted.astype(jnp.float32)
    for block in range(blocks):
        start = block * per_slab * PW
        cut[block] = weighted[:, start : start + reach * PW]

    def cut_copy(to, slot):
        return pltpu.make_async_remote_copy(
            src_ref=cut.at[to], dst_ref=panels.at[slot],
            send_sem=cut_send.at[to], recv_sem=cut_recv.at[slot],
            device_id=(to, gy), device_id_type=MESH,
        )

    def give_cut(step, carry):
        cut_copy(lax.rem(blk + step, blocks), blk).start()
        return carry

    lax.fori_loop(1, blocks, give_cut, 0)
    panels[blk] = cut[blk]

    batch = math.gcd(blocks, 4)

    def back_step(step, carry):
        sources = [lax.rem(blk + step * batch + number, blocks) for number in range(batch)]
        for number, source in enumerate(sources):

            @pl.when(step + number > 0)
            def _():
                cut_copy(source, source).wait_recv()

        for source in sources:
            for t in range(local_tilts):
                shift = shift_rows[pl.ds(source * local_tilts + t, 1), :]
                pieces = []
                for panel in range(window_panels):
                    piece = panels[source, pl.ds(t, 1), pl.ds(panel * PW, PW)]
                    for k in range(1, SHIFTS):
                        moved = panels[source, pl.ds(t, 1), pl.ds((panel + k) * PW, PW)]
                        piece = jnp.where(shift == k, moved, piece)
                    pieces.append(piece)
                rows = band_rows(jnp.concatenate(pieces, axis=1), col_count)
                sheared[:, lanes_of(source, t)] = rows.astype(jnp.bfloat16)
        return carry

    lax.fori_loop(0, blocks // batch, back_step, 0)
    loads[4].wait()
    out_ref[...] += col_ref[...] * lax.dot_general(
        sheared[...], wide[...], (((1,), (1,)), ((), ())), preferred_element_type=jnp.float32
    )

    @pl.when(gy < groups - 1)
    def _():
        tail_copy().wait_send()

    @pl.when(gy > 0)
    def _():
        head_copy().wait_send()

    def settle_line(place, carry):
        block = place * 2 + side
        for tilt in range(local_tilts):

            @pl.when((place <= spot) & can_up)
            def _():
                send_up(block, tilt).wait_send()

            @pl.when((place >= spot) & can_down)
            def _():
                send_down(block, tilt).wait_send()

            near = (place == spot - 1) | (place == spot + 1)

            @pl.when(~near | (tilt < last))
            def _():
                send_side(block, tilt).wait_send()

        return carry

    @pl.when(can_up)
    def _():
        send_up(partner, last).wait_send()

    @pl.when(can_down)
    def _():
        send_down(partner, last).wait_send()

    def settle_blk(step, carry):
        peer = lax.rem(blk + step, blocks)
        send_foot(peer).wait_send()
        cut_copy(peer, blk).wait_send()
        return carry

    def settle_gy(step, carry):
        part_copy(lax.rem(gy + step, groups), gy).wait_send()
        return carry

    lax.fori_loop(0, line, settle_line, 0)
    lax.fori_loop(1, blocks, settle_blk, 0)
    lax.fori_loop(1, groups, settle_gy, 0)


def per_device(blocks, groups, image, measured, row_weight, col_weight, band_weight, band_shift):
    _, col_count, depth = image.shape
    local_tilts, _, band_width = band_weight.shape
    detector_len = measured.shape[2]
    reach = (col_count // PW + SHIFTS) * PW
    window = (blocks, local_tilts, reach)
    dma = pltpu.SemaphoreType.DMA
    units = dma((blocks, local_tilts))
    updated = pl.pallas_call(
        functools.partial(kernel, blocks, groups),
        out_shape=pltpu.VMEM((col_count, depth), jnp.float32),
        in_specs=[pl.BlockSpec(memory_space=pl.ANY)] * 5
        + [pl.BlockSpec(memory_space=pltpu.VMEM)],
        out_specs=pl.BlockSpec(memory_space=pltpu.VMEM),
        scratch_shapes=[
            pltpu.VMEM((col_count, depth), jnp.float32),
            pltpu.VMEM((local_tilts, detector_len), jnp.float32),
            pltpu.VMEM((local_tilts, detector_len), jnp.float32),
            pltpu.VMEM((col_count, depth), jnp.float32),
            pltpu.VMEM((blocks,) + band_weight.shape, jnp.bfloat16),
            pltpu.VMEM((depth, blocks * local_tilts * band_width), jnp.bfloat16),
            pltpu.VMEM((col_count, blocks * local_tilts * band_width), jnp.bfloat16),
            pltpu.VMEM((col_count, depth), jnp.bfloat16),
            pltpu.VMEM((blocks * local_tilts, PW), jnp.int32),
            pltpu.VMEM(window, jnp.float32),
            pltpu.VMEM(window, jnp.float32),
            pltpu.VMEM((groups, local_tilts, detector_len), jnp.float32),
            pltpu.VMEM(window, jnp.float32),
            pltpu.VMEM(window, jnp.float32),
            pltpu.VMEM((2, 8, col_count), jnp.float32),
            pltpu.VMEM((2, PW, col_count), jnp.float32),
            units, units, units, units,
            dma((blocks,)), dma((blocks,)), dma((groups,)), dma((groups,)),
            dma((blocks,)), dma((blocks,)), dma((2,)), dma((2,)), dma((5,)),
        ],
        compiler_params=pltpu.CompilerParams(
            collective_id=0, has_side_effects=True, vmem_limit_bytes=56 * 1024 * 1024
        ),
        cost_estimate=pl.CostEstimate(
            flops=4 * blocks * local_tilts * band_width * col_count * depth,
            bytes_accessed=12 * col_count * depth,
            transcendentals=0,
        ),
    )(image[0], measured[0], row_weight, col_weight, band_weight, band_shift.T)
    return updated[None]


def solution(mesh):
    return jax.shard_map(
        functools.partial(per_device, mesh.shape["blk"], mesh.shape["gy"]),
        mesh=mesh,
        in_specs=(
            P(None, "blk", "gy"),
            P(None, "blk", None),
            P("blk", None),
            P("blk", "gy"),
            P("blk", "gy", None),
            P(),
        ),
        out_specs=P(None, "blk", "gy"),
        check_vma=False,
    )
```

```python
import functools
import math

import jax
import jax.numpy as jnp
from jax import lax
from jax.experimental import pallas as pl
from jax.experimental.pallas import tpu as pltpu
from jax.sharding import PartitionSpec as P

PW = 128
SMOOTH = 0.25
SHIFTS = 4
MESH = pl.DeviceIdType.MESH


def roll_lanes(rows, amount):
    return pltpu.roll(rows, amount % rows.shape[1], 1)


def diagonal_sum(product):
    parts = [product[c : c + PW] for c in range(0, product.shape[0], PW)]
    rows = jnp.concatenate(parts + [jnp.zeros((PW, PW), jnp.float32)], axis=1)
    half = PW // 2
    while half >= 8:
        rows = rows[:half] + roll_lanes(rows[half:], half)
        half //= 2
    sub = lax.broadcasted_iota(jnp.int32, rows.shape, 0)
    for level in (4, 2, 1):
        rows = jnp.where(sub & level != 0, roll_lanes(rows, level), rows)
    return jnp.sum(rows, axis=0, keepdims=True)


def band_rows(line, col_count):
    rows = jnp.broadcast_to(line, (8, line.shape[1]))
    sub = lax.broadcasted_iota(jnp.int32, rows.shape, 0)
    for level in (4, 2, 1):
        rows = jnp.where(sub & level != 0, roll_lanes(rows, -level), rows)
    while rows.shape[0] < PW:
        rows = jnp.concatenate([rows, roll_lanes(rows, -rows.shape[0])], axis=0)
    return jnp.concatenate([rows[:, c : c + PW] for c in range(0, col_count, PW)], axis=0)


def kernel(
    blocks, groups,
    image_hbm, measured_hbm, row_hbm, col_hbm, band_ref, shift_ref, out_ref,
    image_ref, measured_ref, row_ref, col_ref, weights, wide, sheared, copies, shift_rows, placed, footprints, partial, cut, panels, edge_out, edge_in,
    up_sem, down_sem, side_sem, weight_sem,
    foot_send, foot_recv, part_send, part_recv, cut_send, cut_recv, edge_send, edge_recv,
    load_sem,
):
    blk, gy = lax.axis_index("blk"), lax.axis_index("gy")
    line = blocks // 2
    spot, side = blk // 2, blk % 2
    local_tilts, depth, band_width = band_ref.shape
    col_count = image_hbm.shape[0]
    detector_len = measured_ref.shape[1]
    per_slab = col_count // PW
    window_panels = per_slab + 1
    reach = window_panels + SHIFTS - 1

    loads = [
        pltpu.make_async_copy(source, target, load_sem.at[number])
        for number, (source, target) in enumerate(
            [
                (image_hbm, image_ref),
                (band_ref, weights.at[blk]),
                (measured_hbm, measured_ref),
                (row_hbm, row_ref),
                (col_hbm, col_ref),
            ]
        )
    ]
    for load in loads:
        load.start()
    edge_in[...] = jnp.zeros_like(edge_in)
    barrier = pltpu.get_barrier_semaphore()

    def greet_blk(step, carry):
        peer = lax.rem(blk + step, blocks)
        pl.semaphore_signal(barrier, inc=1, device_id=(peer, gy), device_id_type=MESH)
        return carry

    def greet_gy(step, carry):
        peer = lax.rem(gy + step, groups)
        pl.semaphore_signal(barrier, inc=1, device_id=(blk, peer), device_id_type=MESH)
        return carry

    lax.fori_loop(1, blocks, greet_blk, 0)
    lax.fori_loop(1, groups, greet_gy, 0)
    pl.semaphore_wait(barrier, blocks + groups - 2)

    def send_weights(block, tilt, sems, to, source):
        held = weights.at[block, tilt]
        return pltpu.make_async_remote_copy(
            src_ref=held if source is None else source.at[tilt], dst_ref=held,
            send_sem=sems.at[block, tilt], recv_sem=weight_sem.at[block, tilt],
            device_id=(to, gy), device_id_type=MESH,
        )

    def send_up(block, tilt, source=None):
        return send_weights(block, tilt, up_sem, lax.rem(blk + 2, blocks), source)

    def send_down(block, tilt, source=None):
        return send_weights(block, tilt, down_sem, lax.rem(blk + blocks - 2, blocks), source)

    def send_side(block, tilt, source=None):
        return send_weights(block, tilt, side_sem, blk + 1 - 2 * side, source)

    def send_foot(block):
        return pltpu.make_async_remote_copy(
            src_ref=placed.at[block], dst_ref=footprints.at[blk],
            send_sem=foot_send.at[block], recv_sem=foot_recv.at[blk],
            device_id=(block, gy), device_id_type=MESH,
        )

    def foot_from(block):
        return pltpu.make_async_remote_copy(
            src_ref=placed.at[block], dst_ref=footprints.at[block],
            send_sem=foot_send.at[block], recv_sem=foot_recv.at[block],
            device_id=(block, gy), device_id_type=MESH,
        )

    def edge_copy(which, to):
        return pltpu.make_async_remote_copy(
            src_ref=edge_out.at[which], dst_ref=edge_in.at[which, pl.ds(0, 8)],
            send_sem=edge_send.at[which], recv_sem=edge_recv.at[which],
            device_id=(blk, to), device_id_type=MESH,
        )

    def tail_copy():
        return edge_copy(0, lax.rem(gy + 1, groups))

    def head_copy():
        return edge_copy(1, lax.rem(gy + groups - 1, groups))

    last = local_tilts - 1
    can_up, can_down = spot < line - 1, spot > 0
    for tilt in range(local_tilts):

        @pl.when(can_up)
        def _():
            send_up(blk, tilt, band_ref).start()

        @pl.when(can_down)
        def _():
            send_down(blk, tilt, band_ref).start()

        send_side(blk, tilt, band_ref).start()

    loads[0].wait()
    copies[...] = image_ref[...].astype(jnp.bfloat16)
    slab = lax.broadcasted_iota(jnp.int32, shift_ref.shape, 0)
    own_shift = jnp.sum(jnp.where(slab == blk, shift_ref[...], 0), axis=0, keepdims=True)
    square = (blocks * local_tilts, blocks * local_tilts)
    diagonal = lax.broadcasted_iota(jnp.int32, square, 0) == lax.broadcasted_iota(
        jnp.int32, square, 1
    )
    own_shift = jnp.where(diagonal, jnp.broadcast_to(own_shift, square), 0)
    own_shift = jnp.sum(own_shift, axis=1, keepdims=True)
    shift_rows[...] = jnp.broadcast_to(own_shift, shift_rows.shape)

    edge_out[0] = image_ref[:, depth - PW :].T[PW - 8 :]
    edge_out[1] = image_ref[:, :PW].T[:8]

    @pl.when(gy < groups - 1)
    def _():
        tail_copy().start()

    @pl.when(gy > 0)
    def _():
        head_copy().start()

    def lanes_of(block, tilt):
        number = block * local_tilts + tilt
        return pl.ds(pl.multiple_of(number * band_width, band_width), band_width)

    def project(block, tilt):
        band = weights[block, tilt]
        wide[:, lanes_of(block, tilt)] = band
        product = jnp.dot(copies[...], band, preferred_element_type=jnp.float32)
        window = diagonal_sum(product)
        shift = shift_rows[pl.ds(block * local_tilts + tilt, 1), :]
        for panel in range(reach):
            total = jnp.zeros((1, PW), jnp.float32)
            for k in range(SHIFTS):
                if 0 <= panel - k < window_panels:
                    piece = window[:, (panel - k) * PW : (panel - k + 1) * PW]
                    total = jnp.where(shift == k, piece, total)
            placed[block, pl.ds(tilt, 1), pl.ds(panel * PW, PW)] = total
        if tilt < last:
            return

        @pl.when(block != blk)
        def _():
            send_foot(block).start()

        @pl.when(block == blk)
        def _():
            footprints[blk] = placed[blk]

    def smooth():
        @pl.when(gy > 0)
        def _():
            tail_copy().wait_recv()

        @pl.when(gy < groups - 1)
        def _():
            head_copy().wait_recv()

        before = edge_in[0].T[:, 7:8]
        after = edge_in[1].T[:, 0:1]
        chunk = 32
        lane = lax.broadcasted_iota(jnp.int32, (chunk, depth), 1)
        for top in range(0, col_count, chunk):
            rows = slice(top, top + chunk)
            here = image_ref[rows, :]
            left = jnp.where(lane == 0, before[rows], roll_lanes(here, 1))
            right = jnp.where(lane == depth - 1, after[rows], roll_lanes(here, -1))
            out_ref[rows, :] = here + SMOOTH * (left + right - 2.0 * here)

    partner = blk + 1 - 2 * side
    handover = max(line - 1, 2)

    def gather_step(step, carry):
        below, above = spot - step, spot + step

        @pl.when((step == handover) & can_up)
        def _():
            send_up(partner, last).start()

        @pl.when((step == handover) & can_down)
        def _():
            send_down(partner, last).start()

        for tilt in range(local_tilts):
            across = (step > 1) | (tilt < last)

            @pl.when((step > 0) & (below >= 0))
            def _():
                block = below * 2 + side
                send_up(block, tilt).wait_recv()

                @pl.when(can_up)
                def _():
                    send_up(block, tilt).start()

                @pl.when(across)
                def _():
                    send_side(block, tilt).start()

            @pl.when((step > 0) & (above < line))
            def _():
                block = above * 2 + side
                send_down(block, tilt).wait_recv()

                @pl.when(can_down)
                def _():
                    send_down(block, tilt).start()

                @pl.when(across)
                def _():
                    send_side(block, tilt).start()

        def visit(turn, carry):
            kind = turn // 2
            far = jnp.where(kind == 2, 1, step - kind)
            place = jnp.where(turn % 2 == 0, spot - far, spot + far)
            inside = (far >= 0) & (place >= 0) & (place < line) & ((far > 0) | (turn % 2 == 0))
            inside = inside & ((kind < 2) | (step == line))
            block = place * 2 + jnp.where(kind == 0, side, 1 - side)
            late = (kind == 1) & (far == 1)
            for tilt in range(local_tilts):
                wanted = ~late & (kind < 2) if tilt == last else kind < 2
                wanted = wanted | (kind == 2) if tilt == last else wanted

                @pl.when(inside & wanted)
                def _():
                    @pl.when(kind > 0)
                    def _():
                        send_side(block, tilt).wait_recv()

                    project(block, tilt)

            return carry

        lax.fori_loop(0, 6, visit, 0)

        @pl.when(step == line)
        def _():
            smooth()

        return carry

    loads[1].wait()
    lax.fori_loop(0, line + 1, gather_step, 0)

    def take_foot(step, carry):
        foot_from(lax.rem(blk + step, blocks)).wait_recv()
        return carry

    lax.fori_loop(1, blocks, take_foot, 0)

    partial[gy] = jnp.zeros((local_tilts, detector_len), jnp.float32)
    for source in range(blocks):
        bins = pl.ds(source * per_slab * PW, reach * PW)
        partial[gy, :, bins] = partial[gy, :, bins] + footprints[source]

    def part_copy(to, slot):
        return pltpu.make_async_remote_copy(
            src_ref=partial.at[gy], dst_ref=partial.at[slot],
            send_sem=part_send.at[to], recv_sem=part_recv.at[slot],
            device_id=(blk, to), device_id_type=MESH,
        )

    def give_part(step, carry):
        part_copy(lax.rem(gy + step, groups), gy).start()
        return carry

    def take_part(step, carry):
        peer = lax.rem(gy + step, groups)
        part_copy(peer, peer).wait_recv()
        return carry

    lax.fori_loop(1, groups, give_part, 0)
    lax.fori_loop(1, groups, take_part, 0)

    loads[2].wait()
    loads[3].wait()
    projection = partial[0]
    for group in range(1, groups):
        projection = projection + partial[group]
    weighted = (row_ref[...] * (measured_ref[...] - projection)).astype(jnp.bfloat16)
    weighted = weighted.astype(jnp.float32)
    for block in range(blocks):
        start = block * per_slab * PW
        cut[block] = weighted[:, start : start + reach * PW]

    def cut_copy(to, slot):
        return pltpu.make_async_remote_copy(
            src_ref=cut.at[to], dst_ref=panels.at[slot],
            send_sem=cut_send.at[to], recv_sem=cut_recv.at[slot],
            device_id=(to, gy), device_id_type=MESH,
        )

    def give_cut(step, carry):
        cut_copy(lax.rem(blk + step, blocks), blk).start()
        return carry

    lax.fori_loop(1, blocks, give_cut, 0)
    panels[blk] = cut[blk]

    batch = math.gcd(blocks, 4)

    def back_step(step, carry):
        sources = [lax.rem(blk + step * batch + number, blocks) for number in range(batch)]
        for number, source in enumerate(sources):

            @pl.when(step + number > 0)
            def _():
                cut_copy(source, source).wait_recv()

        for source in sources:
            for t in range(local_tilts):
                shift = shift_rows[pl.ds(source * local_tilts + t, 1), :]
                pieces = []
                for panel in range(window_panels):
                    piece = panels[source, pl.ds(t, 1), pl.ds(panel * PW, PW)]
                    for k in range(1, SHIFTS):
                        moved = panels[source, pl.ds(t, 1), pl.ds((panel + k) * PW, PW)]
                        piece = jnp.where(shift == k, moved, piece)
                    pieces.append(piece)
                rows = band_rows(jnp.concatenate(pieces, axis=1), col_count)
                sheared[:, lanes_of(source, t)] = rows.astype(jnp.bfloat16)
        return carry

    def settle_line(place, carry):
        block = place * 2 + side
        for tilt in range(local_tilts):

            @pl.when((place <= spot) & can_up)
            def _():
                send_up(block, tilt).wait_send()

            @pl.when((place >= spot) & can_down)
            def _():
                send_down(block, tilt).wait_send()

            near = (place == spot - 1) | (place == spot + 1)

            @pl.when(~near | (tilt < last))
            def _():
                send_side(block, tilt).wait_send()

        return carry

    @pl.when(can_up)
    def _():
        send_up(partner, last).wait_send()

    @pl.when(can_down)
    def _():
        send_down(partner, last).wait_send()

    lax.fori_loop(0, line, settle_line, 0)
    lax.fori_loop(0, blocks // batch, back_step, 0)
    loads[4].wait()
    out_ref[...] += col_ref[...] * lax.dot_general(
        sheared[...], wide[...], (((1,), (1,)), ((), ())), preferred_element_type=jnp.float32
    )

    @pl.when(gy < groups - 1)
    def _():
        tail_copy().wait_send()

    @pl.when(gy > 0)
    def _():
        head_copy().wait_send()

    def settle_blk(step, carry):
        peer = lax.rem(blk + step, blocks)
        send_foot(peer).wait_send()
        cut_copy(peer, blk).wait_send()
        return carry

    def settle_gy(step, carry):
        part_copy(lax.rem(gy + step, groups), gy).wait_send()
        return carry

    lax.fori_loop(1, blocks, settle_blk, 0)
    lax.fori_loop(1, groups, settle_gy, 0)


def per_device(blocks, groups, image, measured, row_weight, col_weight, band_weight, band_shift):
    _, col_count, depth = image.shape
    local_tilts, _, band_width = band_weight.shape
    detector_len = measured.shape[2]
    reach = (col_count // PW + SHIFTS) * PW
    window = (blocks, local_tilts, reach)
    dma = pltpu.SemaphoreType.DMA
    units = dma((blocks, local_tilts))
    updated = pl.pallas_call(
        functools.partial(kernel, blocks, groups),
        out_shape=pltpu.VMEM((col_count, depth), jnp.float32),
        in_specs=[pl.BlockSpec(memory_space=pl.ANY)] * 5
        + [pl.BlockSpec(memory_space=pltpu.VMEM)],
        out_specs=pl.BlockSpec(memory_space=pltpu.VMEM),
        scratch_shapes=[
            pltpu.VMEM((col_count, depth), jnp.float32),
            pltpu.VMEM((local_tilts, detector_len), jnp.float32),
            pltpu.VMEM((local_tilts, detector_len), jnp.float32),
            pltpu.VMEM((col_count, depth), jnp.float32),
            pltpu.VMEM((blocks,) + band_weight.shape, jnp.bfloat16),
            pltpu.VMEM((depth, blocks * local_tilts * band_width), jnp.bfloat16),
            pltpu.VMEM((col_count, blocks * local_tilts * band_width), jnp.bfloat16),
            pltpu.VMEM((col_count, depth), jnp.bfloat16),
            pltpu.VMEM((blocks * local_tilts, PW), jnp.int32),
            pltpu.VMEM(window, jnp.float32),
            pltpu.VMEM(window, jnp.float32),
            pltpu.VMEM((groups, local_tilts, detector_len), jnp.float32),
            pltpu.VMEM(window, jnp.float32),
            pltpu.VMEM(window, jnp.float32),
            pltpu.VMEM((2, 8, col_count), jnp.float32),
            pltpu.VMEM((2, PW, col_count), jnp.float32),
            units, units, units, units,
            dma((blocks,)), dma((blocks,)), dma((groups,)), dma((groups,)),
            dma((blocks,)), dma((blocks,)), dma((2,)), dma((2,)), dma((5,)),
        ],
        compiler_params=pltpu.CompilerParams(
            collective_id=0, has_side_effects=True, vmem_limit_bytes=56 * 1024 * 1024
        ),
        cost_estimate=pl.CostEstimate(
            flops=4 * blocks * local_tilts * band_width * col_count * depth,
            bytes_accessed=12 * col_count * depth,
            transcendentals=0,
        ),
    )(image[0], measured[0], row_weight, col_weight, band_weight, band_shift.T)
    return updated[None]


def solution(mesh):
    return jax.shard_map(
        functools.partial(per_device, mesh.shape["blk"], mesh.shape["gy"]),
        mesh=mesh,
        in_specs=(
            P(None, "blk", "gy"),
            P(None, "blk", None),
            P("blk", None),
            P("blk", "gy"),
            P("blk", "gy", None),
            P(),
        ),
        out_specs=P(None, "blk", "gy"),
        check_vma=False,
    )
```
